512 devices in a mesh: space: 32 (over z_lo, x), sub: 16 (over z_hi, y, core).
Axes of the slice: x: 4, y: 4, z: 16 (z_hi: 2, z_lo: 8; z = z_hi * 8 + z_lo), core: 2. Of those that a mesh axis runs over, the one named last changes fastest.
Arguments:
- parent_local: bfloat16 [32, 64, 128], P('space'), may hold values from -6 to 6
- poles_mid: bfloat16 [512, 64, 128], P(('space', 'sub')), may hold values from -6 to 6
- poles_fine: bfloat16 [4096, 64, 128], P(('space', 'sub')), may hold values from -6 to 6
- transfer_mid: bfloat16 [189, 64, 64], replicated, may hold values from -0.125 to 0.125
- transfer_fine: bfloat16 [189, 64, 64], replicated, may hold values from -0.0546875 to 0.0546875
- shift_child: bfloat16 [8, 64, 64], replicated, may hold values from -0.75 to 0.75
- lists_mid: int32 [512, 189], P(('space', 'sub')), may hold values from -1 to 511, as said below
- lists_fine: int32 [4096, 189], P(('space', 'sub')), may hold values from -1 to 4095, as said below
- octant_mid: int32 [512], P(('space', 'sub')), may hold values from 0 to 7
- octant_fine: int32 [4096], P(('space', 'sub')), may hold values from 0 to 7
- parent_fine: int32 [4096], P(('space', 'sub')), may hold values from 0 to 511, as said below
Outputs:
- local_fine: bfloat16 [4096, 64, 128], P(('space', 'sub'))
The draws below stay inside these ranges and needn't reach their ends.
Inputs may be any that keep to these rules, and one draw needn't show every extreme that they name: `lists_mid`: the sources named in the list of a level-4 box are distinct, differ from the box itself, and lie in its partition or in the partition just before or after it; a partition holds 16 consecutive level-4 boxes. A list names at least half of min(189, 47), rounded down, sources and at most all the sources it may use. `lists_fine`: the sources named in the list of a level-5 box are distinct, differ from the box itself, and lie in its partition or in the partition just before or after it; a partition holds 128 consecutive level-5 boxes. A list names at least half of min(189, 383), rounded down, sources and at most all the sources it may use. `parent_fine`: each level-4 box is the parent of exactly 8 level-5 boxes, all in its own partition.
All inputs are finite; a program needn't handle non-finite values.
Results may differ from the reference program's by a relative error of at most 0.0045.
Values may be sent and summed in bfloat16 or wider, within the bound.
A program may use at most 128 MiB of HBM per device.

```python
import math
import jax
import jax.numpy as jnp
from jax import lax

COEF = 64
PROBES = 128
CLASSES = 189
BOX4_DEV = 1
BOX5_DEV = 8
PARTS_SIZE = 32
BOXES4 = 512
BOXES5 = 4096
N_SUB = 16


def interaction_table(key, box_count, part_size, dev_size, classes):
    window = 3 * part_size
    key_pick, key_keep, key_shuffle = jax.random.split(key, 3)
    target = jnp.arange(box_count, dtype=jnp.int32)
    slot_ids = jnp.arange(window, dtype=jnp.int32)
    source = (target[:, None] // part_size - 1) * part_size + slot_ids[None, :]
    usable_all = (source >= 0) & (source < box_count) & (source != target[:, None])
    scores = jax.random.randint(key_pick, (box_count, window), 0, 1 << 16) * window + slot_ids[None, :]
    scores = jnp.where(usable_all, scores, scores + (1 << 29))
    ranking = jnp.argsort(scores, axis=1)
    used_cols = min(classes, window)
    chosen = jnp.take_along_axis(source, ranking[:, :used_cols], axis=1)
    usable = jnp.take_along_axis(usable_all, ranking[:, :used_cols], axis=1)
    density = jax.random.randint(key_keep, (box_count // dev_size,), 2, 5)
    kept_count = jnp.repeat(density, dev_size) * used_cols // 4
    usable = usable & (jnp.arange(used_cols, dtype=jnp.int32)[None, :] < kept_count[:, None])
    chosen = jnp.where(usable, chosen, -1).astype(jnp.int32)
    if classes > used_cols:
        chosen = jnp.concatenate([chosen, jnp.full((box_count, classes - used_cols), -1, jnp.int32)], 1)
    shuffle = jax.random.randint(key_shuffle, (box_count, classes), 0, 1 << 16) * classes + jnp.arange(classes, dtype=jnp.int32)[None, :]
    return jnp.take_along_axis(chosen, jnp.argsort(shuffle, axis=1), axis=1).astype(jnp.int32)


def draw_lists_mid(key, part):
    key = jax.random.fold_in(key, 11)
    return interaction_table(key, BOXES4, BOXES4 // PARTS_SIZE, BOX4_DEV, CLASSES)


def draw_lists_fine(key, part):
    key = jax.random.fold_in(key, 12)
    return interaction_table(key, BOXES5, BOXES5 // PARTS_SIZE, BOX5_DEV, CLASSES)


def draw_parent_fine(key, part):
    key = jax.random.fold_in(key, 13)
    mid_size = BOXES4 // PARTS_SIZE
    fine_size = BOXES5 // PARTS_SIZE
    scores = jax.random.randint(key, (PARTS_SIZE, fine_size), 0, 1 << 16) * fine_size + jnp.arange(fine_size, dtype=jnp.int32)[None, :]
    permuted = jnp.argsort(scores, axis=1).astype(jnp.int32)
    parents = jnp.arange(PARTS_SIZE, dtype=jnp.int32)[:, None] * mid_size + permuted // 8
    return parents.reshape(BOXES5).astype(jnp.int32)


def place_ends(array, stream_key, smallest, high):
    place = [jax.random.randint(jax.random.fold_in(stream_key, axis), (), 0, length) for axis, length in enumerate(array.shape)]
    longest = array.shape.index(max(array.shape))
    neighbour = place[:longest] + [(place[longest] + 1) % array.shape[longest]] + place[longest + 1:]
    return array.at[tuple(place)].set(smallest).at[tuple(neighbour)].set(high)


def levels(key, extent, pieces, least, top_value):
    def one(axis_at, blocks):
        steps = jax.random.uniform(jax.random.fold_in(jax.random.fold_in(key, 6), axis_at), (blocks,), jnp.float32, least / len(pieces), top_value / len(pieces))
        return jnp.repeat(jnp.exp(steps), extent[axis_at] // blocks).reshape((-1,) + (1,) * (len(extent) - axis_at - 1))

    loudness = one(*pieces[0])
    for cut in pieces[1:]:
        loudness = loudness * one(*cut)
    return loudness


def scatter_about(rng, dims, width, limit, cuts=(), held_as=jnp.bfloat16):
    values = jax.random.normal(rng, dims, jnp.float32) * width
    if len(cuts) > 0:
        values = levels(rng, dims, cuts, -0.22, 0.18) * values
    return jnp.clip(values, min=-limit, max=limit).astype(held_as)


def setup_inputs(seed: int = 0) -> dict:
    key_of = jax.random.split(jax.random.key(seed), 12)
    parent_local = scatter_about(key_of[0], (PARTS_SIZE, COEF, PROBES), 1.0, 6.0, ((0, 32),))
    poles_mid = scatter_about(key_of[1], (BOXES4, COEF, PROBES), 1.0, 6.0, ((0, 512),))
    poles_fine = scatter_about(key_of[2], (BOXES5, COEF, PROBES), 1.0, 6.0, ((0, 512),))
    transfer_mid = scatter_about(key_of[3], (CLASSES, COEF, COEF), (2 * N_SUB * BOX4_DEV * COEF) ** -0.5, 0.125)
    transfer_fine = scatter_about(key_of[4], (CLASSES, COEF, COEF), (CLASSES * COEF) ** -0.5, 0.0546875)
    shift_child = scatter_about(key_of[5], (8, COEF, COEF), COEF ** -0.5, 0.75)
    lists_mid = draw_lists_mid(jax.random.fold_in(key_of[11], 71), 0)
    lists_fine = draw_lists_fine(jax.random.fold_in(key_of[11], 71), 0)
    octant_mid = place_ends(jax.random.randint(key_of[8], (BOXES4,), 0, 8), jax.random.fold_in(key_of[8], 1), 0, 7).astype(jnp.int32)
    octant_fine = place_ends(jax.random.randint(key_of[9], (BOXES5,), 0, 8), jax.random.fold_in(key_of[9], 1), 0, 7).astype(jnp.int32)
    parent_fine = draw_parent_fine(jax.random.fold_in(key_of[11], 71), 0)
    return {"parent_local": parent_local, "poles_mid": poles_mid, "poles_fine": poles_fine, "transfer_mid": transfer_mid, "transfer_fine": transfer_fine, "shift_child": shift_child, "lists_mid": lists_mid, "lists_fine": lists_fine, "octant_mid": octant_mid, "octant_fine": octant_fine, "parent_fine": parent_fine}


def far_field(operators, panels, lists):
    box_count = lists.shape[0]
    stride = math.gcd(box_count, 8)
    wide_ops = operators.astype(jnp.float32)

    def translate_block(entries):
        present = entries >= 0
        picked = panels[jnp.where(present, entries, 0)].astype(jnp.float32)
        picked = jnp.where(present[:, :, None, None], picked, jnp.float32(0.0))
        return jnp.einsum('cij,gcjn->gin', wide_ops, picked)

    result = lax.map(translate_block, lists.reshape(box_count // stride, stride, lists.shape[1]))
    return result.reshape(box_count, panels.shape[1], panels.shape[2])


def child_shift(shift_child, octants, parents):
    chosen = shift_child[octants].astype(jnp.float32)
    return jnp.einsum('bij,bjn->bin', chosen, parents.astype(jnp.float32))


def reference(parent_local, poles_mid, poles_fine, transfer_mid, transfer_fine, shift_child, lists_mid, lists_fine, octant_mid, octant_fine, parent_fine):
    per_part = BOXES4 // PARTS_SIZE
    owners = (jnp.arange(BOXES4, dtype=jnp.int32) // per_part).astype(jnp.int32)
    far_mid = far_field(transfer_mid, poles_mid, lists_mid)
    level_mid = (child_shift(shift_child, octant_mid, parent_local[owners]) + far_mid).astype(jnp.bfloat16)
    far_fine = far_field(transfer_fine, poles_fine, lists_fine)
    local_fine = child_shift(shift_child, octant_fine, level_mid[parent_fine]) + far_fine
    return local_fine.astype(jnp.bfloat16)
```

```python
import functools

import jax
import jax.numpy as jnp
from jax import lax
from jax.experimental import pallas as pl
from jax.experimental.pallas import tpu as pltpu
from jax.sharding import PartitionSpec as P

MESH = pl.DeviceIdType.MESH
FAR = 189
SHIFT = 192
HALF = 100
FINE_STEPS, FINE_WORDS = 10, 10
MID_STEPS, MID_WORDS = 4, 25
ZERO_FINE, MID_FINE = 384, 385
ZERO_MID, PARENT_MID = 48, 49


def kernel(
    parent_ref,
    mid_ref,
    fine_ref,
    tmid_hbm,
    tfine_hbm,
    shift_hbm,
    lmid_ref,
    lfine_ref,
    omid_ref,
    ofine_ref,
    pfine_ref,
    out_ref,
    ops_fine,
    ops_mid,
    w_fine,
    w_mid,
    stage,
    raw,
    table,
    table_mid,
    ext,
    words,
    steps_fine,
    steps_mid,
    flipped,
    level,
    level_in,
    result,
    result_in,
    sm_even,
    sm_odd,
    sm_mid,
    op_sem,
    sm_sem,
    a2a_send,
    a2a_recv,
    list_send,
    list_recv,
    twin_send,
    twin_recv,
    side_send,
    side_recv,
    level_send,
    level_recv,
    out_send,
    out_recv,
):
    space = lax.axis_index("space")
    sub = lax.axis_index("sub")
    core = sub % 2
    group = sub // 2
    z_hi = group // 4
    y = group % 4
    twin = (space, group * 2 + 1 - core)

    owners = [(1 - z_hi) * 4 + (y + j) % 4 for j in range(4)]
    owners += [z_hi * 4 + (y + j) % 4 for j in range(4)]
    OWN = 4

    def peer(owner):
        return (space, owner * 2 + core)

    def remote(src, dst, send, recv, device):
        return pltpu.make_async_remote_copy(
            src_ref=src, dst_ref=dst, send_sem=send, recv_sem=recv, device_id=device, device_id_type=MESH
        )

    barrier = pltpu.get_barrier_semaphore()
    for j in range(8):
        if j != OWN:
            pl.semaphore_signal(barrier, inc=1, device_id=peer(owners[j]), device_id_type=MESH)
    pl.semaphore_signal(barrier, inc=1, device_id=twin, device_id_type=MESH)

    @pl.when(space > 0)
    def _():
        pl.semaphore_signal(barrier, inc=1, device_id=(space - 1, sub), device_id_type=MESH)

    @pl.when(space < 31)
    def _():
        pl.semaphore_signal(barrier, inc=1, device_id=(space + 1, sub), device_id_type=MESH)

    op_copies = [
        pltpu.make_async_copy(tmid_hbm, ops_mid.at[pl.ds(0, FAR)], op_sem.at[0]),
        pltpu.make_async_copy(shift_hbm, ops_mid.at[pl.ds(SHIFT, 8)], op_sem.at[1]),
        pltpu.make_async_copy(tfine_hbm, ops_fine.at[pl.ds(0, FAR)], op_sem.at[2]),
        pltpu.make_async_copy(shift_hbm, ops_fine.at[pl.ds(SHIFT, 8)], op_sem.at[3]),
    ]
    for c in op_copies:
        c.start()

    low = lax.broadcasted_iota(jnp.int32, (8, 128), 1) < 64
    for i in range(4):
        pair = fine_ref[2 * i : 2 * i + 2].reshape(128, 128).astype(jnp.float32).T
        for g in range(8):
            a = pair[16 * g : 16 * g + 8]
            b = pair[16 * g + 8 : 16 * g + 16]
            first = jnp.where(low, a, pltpu.roll(b, 64, 1))
            second = jnp.where(low, pltpu.roll(a, 64, 1), b)
            stage[g, 16 * i : 16 * i + 16] = jnp.concatenate([first, second], 0).astype(jnp.bfloat16)

    def doubled(panel):
        panel = panel.astype(jnp.float32)
        return jnp.concatenate([panel, panel], 0).T

    box = doubled(mid_ref[0])
    for g in range(8):
        rows = jnp.where(low, box[16 * g : 16 * g + 8], box[16 * g + 8 : 16 * g + 16])
        stage[g, 64:80] = jnp.concatenate([rows, jnp.zeros_like(rows)], 0).astype(jnp.bfloat16)
    flipped[...] = doubled(parent_ref[0])

    ext[0:8, 0:FAR] = lfine_ref[...]
    ext[8:9, 0:FAR] = lmid_ref[...]
    entry = ext[...]
    row = lax.broadcasted_iota(jnp.int32, (16, 256), 0)
    lane = lax.broadcasted_iota(jnp.int32, (16, 256), 1)
    octant = jnp.where(row == 8, omid_ref[0], -1)
    parent = jnp.where(row == 8, PARENT_MID, 0)
    for t in range(8):
        octant = jnp.where(row == t, ofine_ref[t], octant)
        parent = jnp.where(row == t, MID_FINE + jnp.clip(pfine_ref[t] - space * 16, 0, 15), parent)
    nothing = jnp.where(row < 8, ZERO_FINE, ZERO_MID)
    start = jnp.where(row < 8, (space - 1) * 128, (space - 1) * 16)
    last = jnp.where(row < 8, ZERO_FINE, ZERO_MID) - 1
    far = jnp.where(entry >= 0, jnp.clip(entry - start, 0, last), nothing)
    near = jnp.where(lane - SHIFT == octant, parent, nothing)
    rows = jnp.where(lane < FAR, far, near)
    packed = rows[:, :128] + pltpu.roll(rows, 256 - HALF, 1)[:, :128] * 65536
    for j in [OWN]:
        words[owners[j]] = packed

    pl.semaphore_wait(barrier, 8 + (space + 31) // 32 + (62 - space) // 32)

    own = owners[OWN]
    for j in range(8):
        if j != OWN:
            o = owners[j]
            remote(words.at[own], words.at[own], list_send.at[o], list_recv.at[own], peer(o)).start()
            remote(stage.at[o], raw.at[1, core, own], a2a_send.at[o], a2a_recv.at[own], peer(o)).start()
    raw[1, core, own] = stage[own]

    def forward(o):
        piece = raw.at[1, core, o]
        remote(piece, piece, twin_send.at[1, o], twin_recv.at[1, o], twin).start()

        @pl.when(space < 31)
        def _():
            remote(
                piece, raw.at[0, core, o], side_send.at[0, o], side_recv.at[0, o], (space + 1, sub)
            ).start()

        @pl.when(space > 0)
        def _():
            remote(
                piece, raw.at[2, core, o], side_send.at[1, o], side_recv.at[1, o], (space - 1, sub)
            ).start()

    def fill(rel, c, o):
        first = rel * 128 + (o * 2 + c) * 8
        piece = raw[rel, c, o].astype(jnp.float32)
        table[pl.ds(first, 8)] = piece[0:64].reshape(8, 8, 128)
        mid = rel * 16 + o * 2 + c
        table_mid[mid] = piece[64:72]

    forward(own)
    fill(1, core, own)

    for c in op_copies:
        c.wait()
    blank = jnp.zeros((64, 64), jnp.bfloat16)
    for ops, w, steps, count in (
        (ops_mid, w_mid, MID_STEPS, MID_WORDS),
        (ops_fine, w_fine, FINE_STEPS, FINE_WORDS),
    ):
        for c in range(FAR, SHIFT):
            ops[c] = blank

        def lay(m, carry, ops=ops, w=w, count=count):
            for q in range(count):
                for h in range(2):
                    op = ops[m * count + q + HALF * h]
                    at = (2 * q + h) * 128
                    w[m, 0:64, at : at + 128] = jnp.concatenate([op, blank], 1)
                    w[m, 64:128, at : at + 128] = jnp.concatenate([blank, op], 1)
            return carry

        lax.fori_loop(0, steps, lay, 0)

    table[ZERO_FINE] = jnp.zeros((8, 128), jnp.float32)
    table_mid[ZERO_MID] = jnp.zeros((8, 128), jnp.float32)
    at = pl.multiple_of(group * 16, 16)
    table_mid[PARENT_MID] = jnp.where(
        low, flipped[pl.ds(at, 8), :], flipped[pl.ds(at + 8, 8), :]
    )

    def arrive(o):
        piece = raw.at[1, core, o]
        remote(piece, piece, a2a_send.at[o], a2a_recv.at[o], twin).wait_recv()
        forward(o)
        fill(1, core, o)

    def arrive_side(o):
        for side, rel, there in ((0, 0, space > 0), (1, 2, space < 31)):

            @pl.when(there)
            def _(side=side, rel=rel):
                piece = raw.at[rel, core, o]
                remote(piece, piece, side_send.at[side, o], side_recv.at[side, o], twin).wait_recv()
                remote(piece, piece, twin_send.at[rel, o], twin_recv.at[rel, o], twin).start()
                fill(rel, core, o)

    for j in (5, 6, 7):
        arrive(owners[j])
    for j in (4, 5, 6, 7):
        arrive_side(owners[j])

    for j in range(8):
        if j != OWN:
            o = owners[j]
            remote(words.at[o], words.at[o], list_send.at[o], list_recv.at[o], twin).wait_recv()
    lists = [words[o] for o in owners]
    flat = jnp.concatenate(
        [v[0:8] for v in lists] + [v[8:9] for v in lists] + [jnp.zeros((56, 128), jnp.int32)], 0
    ).T
    for tile in range(2):
        part = pltpu.roll(flat, 128 - 32 * tile, 1) if tile else flat
        for m in range(FINE_STEPS):
            steps_fine[tile, m, 0:FINE_WORDS] = part[m * FINE_WORDS : (m + 1) * FINE_WORDS]
    part = pltpu.roll(flat, 64, 1)
    for m in range(MID_STEPS):
        steps_mid[m, 0:MID_WORDS] = part[m * MID_WORDS : (m + 1) * MID_WORDS]
    mid_lists = pltpu.make_async_copy(steps_mid, sm_mid, sm_sem.at[2])
    mid_lists.start()

    for j in range(4):
        arrive(owners[j])
    for j in range(4):
        arrive_side(owners[j])
    for j in (4, 5, 6, 7, 0, 1, 2, 3):
        o = owners[j]
        for rel, there in ((1, None), (0, space > 0), (2, space < 31)):

            def take(rel=rel, o=o):
                piece = raw.at[rel, 1 - core, o]
                remote(piece, piece, twin_send.at[rel, o], twin_recv.at[rel, o], twin).wait_recv()
                fill(rel, 1 - core, o)

            if there is None:
                take()
            else:
                pl.when(there)(take)

    def product(source, word, targets, count, weights, acc):
        columns = []
        for q in range(count):
            pair = [word(q, t) for t in range(targets)]
            for row in ([v & 0xFFFF for v in pair], [v >> 16 for v in pair]):
                picked = [source[r] for r in row]
                columns.append(jnp.concatenate(picked, 0).astype(jnp.bfloat16))
        return acc + lax.dot_general(
            jnp.concatenate(columns, 1),
            weights,
            (((1,), (1,)), ((), ())),
            preferred_element_type=jnp.float32,
        )

    mid_lists.wait()
    acc = jnp.zeros((64, 128), jnp.float32)
    for m in range(MID_STEPS):
        acc = product(table_mid, lambda q, t, m=m: sm_mid[m, q, t], 8, MID_WORDS, w_mid[m], acc)
    level[...] = acc.astype(jnp.bfloat16)
    to_twin = remote(level, level_in, level_send.at[0], level_recv.at[0], twin)
    to_twin.start()

    def keep(rows, c):
        rows = rows.astype(jnp.float32)
        for j in range(8):
            table[MID_FINE + owners[j] * 2 + c] = rows[8 * j : 8 * j + 8]

    keep(level[...], core)

    for tile in range(2):

        def load(m, buf, k, tile=tile):
            return pltpu.make_async_copy(steps_fine.at[tile, m], buf, sm_sem.at[k])

        load(0, sm_even, 0).start()

        def body(h, acc, tile=tile, load=load):
            if tile == 0:

                @pl.when(h == FINE_STEPS // 2 - 1)
                def _():
                    to_twin.wait_recv()
                    keep(level_in[...], 1 - core)

            load(2 * h, sm_even, 0).wait()
            load(2 * h + 1, sm_odd, 1).start()
            acc = product(
                table, lambda q, t: sm_even[q, t], 32, FINE_WORDS, w_fine[2 * h], acc
            )
            load(2 * h + 1, sm_odd, 1).wait()

            @pl.when(h < FINE_STEPS // 2 - 1)
            def _():
                load(2 * h + 2, sm_even, 0).start()

            return product(
                table, lambda q, t: sm_odd[q, t], 32, FINE_WORDS, w_fine[2 * h + 1], acc
            )

        acc = lax.fori_loop(0, FINE_STEPS // 2, body, jnp.zeros((256, 128), jnp.float32))
        result[tile] = acc.astype(jnp.bfloat16).reshape(4, 64, 128)
        for i in range(4):
            j = 4 * tile + i
            if j != OWN:
                remote(
                    result.at[tile, i], result_in.at[own], out_send.at[j], out_recv.at[own], peer(owners[j])
                ).start()
    result_in[own] = result[1, 0]

    for j in (0, 1, 2, 3, 5, 6, 7):
        o = owners[j]
        remote(result.at[0, 0], result_in.at[o], out_send.at[j], out_recv.at[o], twin).wait_recv()
    for i in range(4):
        rows = []
        for g in range(8):
            both = result_in[g, 16 * i : 16 * i + 16].astype(jnp.float32)
            a, b = both[0:8], both[8:16]
            rows.append(jnp.where(low, a, pltpu.roll(b, 64, 1)))
            rows.append(jnp.where(low, pltpu.roll(a, 64, 1), b))
        out_ref[2 * i : 2 * i + 2] = (
            jnp.concatenate(rows, 0).T.astype(jnp.bfloat16).reshape(2, 64, 128)
        )

    to_twin.wait_send()
    for j in range(8):
        o = owners[j]
        piece = raw.at[1, core, o]
        if j != OWN:
            remote(words.at[o], words.at[o], list_send.at[o], list_recv.at[o], twin).wait_send()
            remote(piece, piece, a2a_send.at[o], a2a_recv.at[o], twin).wait_send()
            remote(result.at[0, 0], result_in.at[o], out_send.at[j], out_recv.at[o], twin).wait_send()
        remote(piece, piece, twin_send.at[1, o], twin_recv.at[1, o], twin).wait_send()
        for side, rel, there, back in ((0, 0, space < 31, space > 0), (1, 2, space > 0, space < 31)):

            @pl.when(there)
            def _(side=side, o=o, piece=piece):
                remote(piece, piece, side_send.at[side, o], side_recv.at[side, o], twin).wait_send()

            @pl.when(back)
            def _(rel=rel, o=o, piece=piece):
                remote(piece, piece, twin_send.at[rel, o], twin_recv.at[rel, o], twin).wait_send()


def body(*args):
    vmem = pl.BlockSpec(memory_space=pltpu.VMEM)
    smem = pl.BlockSpec(memory_space=pltpu.SMEM)
    hbm = pl.BlockSpec(memory_space=pl.ANY)
    bf16, f32, i32 = jnp.bfloat16, jnp.float32, jnp.int32
    dma = pltpu.SemaphoreType.DMA
    return pl.pallas_call(
        kernel,
        out_shape=jax.ShapeDtypeStruct((8, 64, 128), bf16),
        in_specs=[vmem, vmem, vmem, hbm, hbm, hbm, vmem, vmem, smem, smem, smem],
        out_specs=vmem,
        scratch_shapes=[
            pltpu.VMEM((200, 64, 64), bf16),
            pltpu.VMEM((200, 64, 64), bf16),
            pltpu.VMEM((FINE_STEPS, 128, FINE_WORDS * 256), bf16),
            pltpu.VMEM((MID_STEPS, 128, MID_WORDS * 256), bf16),
            pltpu.VMEM((8, 80, 128), bf16),
            pltpu.VMEM((3, 2, 8, 80, 128), bf16),
            pltpu.VMEM((MID_FINE + 16, 8, 128), f32),
            pltpu.VMEM((PARENT_MID + 1, 8, 128), f32),
            pltpu.VMEM((16, 256), i32),
            pltpu.VMEM((8, 16, 128), i32),
            pltpu.VMEM((2, FINE_STEPS, 16, 128), i32),
            pltpu.VMEM((MID_STEPS, 32, 128), i32),
            pltpu.VMEM((128, 128), f32),
            pltpu.VMEM((64, 128), bf16),
            pltpu.VMEM((64, 128), bf16),
            pltpu.VMEM((2, 4, 64, 128), bf16),
            pltpu.VMEM((8, 64, 128), bf16),
            pltpu.SMEM((16, 128), i32),
            pltpu.SMEM((16, 128), i32),
            pltpu.SMEM((MID_STEPS, 32, 128), i32),
            dma((4,)),
            dma((3,)),
            dma((8,)),
            dma((8,)),
            dma((8,)),
            dma((8,)),
            dma((3, 8)),
            dma((3, 8)),
            dma((2, 8)),
            dma((2, 8)),
            dma((1,)),
            dma((1,)),
            dma((8,)),
            dma((8,)),
        ],
        compiler_params=pltpu.CompilerParams(
            collective_id=0, has_side_effects=True, vmem_limit_bytes=48 * 2**20
        ),
    )(*args)


def solution(mesh):
    placed = (
        P("space", None, None),
        P(("space", "sub"), None, None),
        P(("space", "sub"), None, None),
        P(),
        P(),
        P(),
        P(("space", "sub"), None),
        P(("space", "sub"), None),
        P(("space", "sub")),
        P(("space", "sub")),
        P(("space", "sub")),
    )
    return jax.shard_map(
        body, mesh=mesh, in_specs=placed, out_specs=P(("space", "sub"), None, None), check_vma=False
    )
```

```python
import functools

import jax
import jax.numpy as jnp
from jax import lax
from jax.experimental import pallas as pl
from jax.experimental.pallas import tpu as pltpu
from jax.sharding import PartitionSpec as P

MESH = pl.DeviceIdType.MESH
FAR = 189
SHIFT = 192
HALF = 100
STEPS, WORDS = 4, 25
SPARE = 13
ZERO_FINE, MID_FINE = 384, 385
ZERO_MID, PARENT_MID = 48, 49


def kernel(
    parent_hbm,
    mid_hbm,
    fine_hbm,
    tmid_hbm,
    tfine_hbm,
    shift_hbm,
    lmid_hbm,
    lfine_hbm,
    omid_hbm,
    ofine_hbm,
    pfine_hbm,
    out_ref,
    parent_ref,
    mid_ref,
    fine_ref,
    shift_ref,
    lmid_ref,
    lfine_ref,
    omid_ref,
    ofine_ref,
    pfine_ref,
    ops_fine,
    ops_mid,
    turned,
    shift_wide,
    w_fine,
    w_mid,
    stage,
    raw,
    table,
    table_mid,
    ext,
    words,
    steps_fine,
    steps_mid,
    flipped,
    unpermuted,
    level,
    level_in,
    result,
    result_in,
    sm_fine,
    sm_mid,
    op_sem,
    sm_sem,
    a2a_send,
    a2a_recv,
    list_send,
    list_recv,
    twin_send,
    twin_recv,
    side_send,
    side_recv,
    level_send,
    level_recv,
    out_send,
    out_recv,
):
    space = lax.axis_index("space")
    sub = lax.axis_index("sub")
    core = sub % 2
    group = sub // 2
    z_hi = group // 4
    y = group % 4
    twin = (space, group * 2 + 1 - core)

    owners = [(1 - z_hi) * 4 + (y + j) % 4 for j in range(4)]
    owners += [z_hi * 4 + (y + j) % 4 for j in range(4)]
    OWN = 4

    def peer(owner):
        return (space, owner * 2 + core)

    def remote(src, dst, send, recv, device):
        return pltpu.make_async_remote_copy(
            src_ref=src, dst_ref=dst, send_sem=send, recv_sem=recv, device_id=device, device_id_type=MESH
        )

    barrier = pltpu.get_barrier_semaphore()
    for j in range(8):
        if j != OWN:
            pl.semaphore_signal(barrier, inc=1, device_id=peer(owners[j]), device_id_type=MESH)
    pl.semaphore_signal(barrier, inc=1, device_id=twin, device_id_type=MESH)

    @pl.when(space > 0)
    def _():
        pl.semaphore_signal(barrier, inc=1, device_id=(space - 1, sub), device_id_type=MESH)

    @pl.when(space < 31)
    def _():
        pl.semaphore_signal(barrier, inc=1, device_id=(space + 1, sub), device_id_type=MESH)

    copies = (
        (fine_hbm, fine_ref),
        (mid_hbm, mid_ref),
        (lfine_hbm, lfine_ref),
        (lmid_hbm, lmid_ref),
        (omid_hbm, omid_ref),
        (ofine_hbm, ofine_ref),
        (pfine_hbm, pfine_ref),
        (parent_hbm, parent_ref),
        (shift_hbm, shift_ref),
        (tmid_hbm, ops_mid),
        (tfine_hbm, ops_fine),
    )
    copies = [pltpu.make_async_copy(a, b, op_sem.at[i]) for i, (a, b) in enumerate(copies)]
    for c in copies:
        c.start()
    for c in copies[:8]:
        c.wait()

    low = lax.broadcasted_iota(jnp.int32, (8, 128), 1) < 64
    for i in range(4):
        pair = fine_ref[2 * i : 2 * i + 2].reshape(128, 128).astype(jnp.float32).T
        for g in range(8):
            a = pair[16 * g : 16 * g + 8]
            b = pair[16 * g + 8 : 16 * g + 16]
            first = jnp.where(low, a, pltpu.roll(b, 64, 1))
            second = jnp.where(low, pltpu.roll(a, 64, 1), b)
            stage[g, 16 * i : 16 * i + 16] = jnp.concatenate([first, second], 0).astype(jnp.bfloat16)

    def doubled(panel):
        panel = panel.astype(jnp.float32)
        return jnp.concatenate([panel, panel], 0).T

    box = doubled(mid_ref[0])
    for g in range(8):
        rows = jnp.where(low, box[16 * g : 16 * g + 8], box[16 * g + 8 : 16 * g + 16])
        stage[g, 64:80] = jnp.concatenate([rows, jnp.zeros_like(rows)], 0).astype(jnp.bfloat16)
    flipped[...] = doubled(parent_ref[0])

    ext[0:8, 0:FAR] = lfine_ref[...]
    ext[8:9, 0:FAR] = lmid_ref[...]
    entry = ext[...]
    row = lax.broadcasted_iota(jnp.int32, (16, 256), 0)
    lane = lax.broadcasted_iota(jnp.int32, (16, 256), 1)
    octant = jnp.where(row == 8, omid_ref[0], -1)
    parent = jnp.where(row == 8, PARENT_MID, 0)
    for t in range(8):
        octant = jnp.where(row == t, ofine_ref[t], octant)
        parent = jnp.where(row == t, MID_FINE + jnp.clip(pfine_ref[t] - space * 16, 0, 15), parent)
    nothing = jnp.where(row < 8, ZERO_FINE, ZERO_MID)
    start = jnp.where(row < 8, (space - 1) * 128, (space - 1) * 16)
    last = jnp.where(row < 8, ZERO_FINE, ZERO_MID) - 1
    far = jnp.where(entry >= 0, jnp.clip(entry - start, 0, last), nothing)
    near = jnp.where(lane - SHIFT == octant, parent, nothing)
    rows = jnp.where(lane < FAR, far, near)
    packed = rows[:, :128] + pltpu.roll(rows, 256 - HALF, 1)[:, :128] * 65536
    fine_words = packed[0:8]
    mid_words = jnp.broadcast_to(packed[8:9], (8, 128))
    row8 = lax.broadcasted_iota(jnp.int32, (8, 128), 0)
    lane8 = lax.broadcasted_iota(jnp.int32, (8, 128), 1)
    spare = (lane8 >= HALF) & (lane8 < HALF + SPARE)
    for r in range(8):
        moved = pltpu.roll(mid_words, (HALF - SPARE * r) % 128, 1)
        fine_words = jnp.where(spare & (row8 == r), moved, fine_words)
    words[owners[OWN]] = fine_words

    pl.semaphore_wait(barrier, 8 + (space + 31) // 32 + (62 - space) // 32)

    own = owners[OWN]
    for j in range(8):
        if j != OWN:
            o = owners[j]
            remote(words.at[own], words.at[own], list_send.at[o], list_recv.at[own], peer(o)).start()
            remote(stage.at[o], raw.at[1, core, own], a2a_send.at[o], a2a_recv.at[own], peer(o)).start()
    raw[1, core, own] = stage[own]

    def forward(o):
        piece = raw.at[1, core, o]
        remote(piece, piece, twin_send.at[1, o], twin_recv.at[1, o], twin).start()

        @pl.when(space < 31)
        def _():
            remote(
                piece, raw.at[0, core, o], side_send.at[0, o], side_recv.at[0, o], (space + 1, sub)
            ).start()

        @pl.when(space > 0)
        def _():
            remote(
                piece, raw.at[2, core, o], side_send.at[1, o], side_recv.at[1, o], (space - 1, sub)
            ).start()

    def fill(rel, c, o):
        first = rel * 128 + (o * 2 + c) * 8
        piece = raw[rel, c, o].astype(jnp.float32)
        table[pl.ds(first, 8)] = piece[0:64].reshape(8, 8, 128)
        mid = rel * 16 + o * 2 + c
        table_mid[mid] = piece[64:72]

    forward(own)
    fill(1, core, own)

    copies[8].wait()
    shift_wide[...] = shift_ref[...].astype(jnp.float32).reshape(512, 64)
    low32 = lax.broadcasted_iota(jnp.int32, (32, 128), 1) < 64

    def operators(ops, w):
        def turn(p, carry):
            both = ops[pl.ds(2 * p, 2)].reshape(128, FAR).astype(jnp.float32)
            at = pl.multiple_of(p * 200, 8)
            turned[pl.ds(at, 128), :] = both[:, 0:128].T
            turned[pl.ds(at + 128, FAR - 128), :] = both[:, 128:FAR].T
            return carry

        lax.fori_loop(0, 32, turn, 0)
        for c in range(FAR, SHIFT):
            turned[pl.ds(c, 32, 200), :] = jnp.zeros((32, 128), jnp.float32)
        for o in range(8):
            even = shift_wide[pl.ds(64 * o, 32, 2), :]
            odd = shift_wide[pl.ds(64 * o + 1, 32, 2), :]
            turned[pl.ds(SHIFT + o, 32, 200), :] = jnp.concatenate([even, odd], 1)

        def lay(m, carry):
            for q in range(WORDS):
                for h in range(2):
                    op = turned[pl.ds(m * WORDS + q + HALF * h, 32, 200), :]
                    swapped = pltpu.roll(op, 64, 1)
                    parts = [
                        jnp.where(low32, op, 0.0),
                        jnp.where(low32, swapped, 0.0),
                        jnp.where(low32, 0.0, swapped),
                        jnp.where(low32, 0.0, op),
                    ]
                    at = (2 * q + h) * 128
                    w[m, :, at : at + 128] = jnp.concatenate(parts, 0).astype(jnp.bfloat16)
            return carry

        lax.fori_loop(0, STEPS, lay, 0)

    copies[9].wait()
    operators(ops_mid, w_mid)

    table[ZERO_FINE] = jnp.zeros((8, 128), jnp.float32)
    table_mid[ZERO_MID] = jnp.zeros((8, 128), jnp.float32)
    at = pl.multiple_of(group * 16, 16)
    table_mid[PARENT_MID] = jnp.where(
        low, flipped[pl.ds(at, 8), :], flipped[pl.ds(at + 8, 8), :]
    )

    def arrive(o):
        piece = raw.at[1, core, o]
        remote(piece, piece, a2a_send.at[o], a2a_recv.at[o], twin).wait_recv()
        forward(o)
        fill(1, core, o)

    def arrive_side(o):
        for side, rel, there in ((0, 0, space > 0), (1, 2, space < 31)):

            @pl.when(there)
            def _(side=side, rel=rel):
                piece = raw.at[rel, core, o]
                remote(piece, piece, side_send.at[side, o], side_recv.at[side, o], twin).wait_recv()
                remote(piece, piece, twin_send.at[rel, o], twin_recv.at[rel, o], twin).start()
                fill(rel, core, o)

    for j in (5, 6, 7):
        arrive(owners[j])
    for j in (4, 5, 6, 7):
        arrive_side(owners[j])
    copies[10].wait()
    operators(ops_fine, w_fine)

    for j in range(8):
        if j != OWN:
            o = owners[j]
            remote(words.at[o], words.at[o], list_send.at[o], list_recv.at[o], twin).wait_recv()
    flat = jnp.concatenate([words[o] for o in owners] + [jnp.zeros((64, 128), jnp.int32)], 0).T
    lane13 = lax.broadcasted_iota(jnp.int32, (SPARE, 128), 1)
    halves = (flat & 0xFFFF, flat >> 16)
    for tile in range(2):
        for m in range(STEPS):
            rows = [v[m * WORDS : (m + 1) * WORDS] for v in halves]
            rows = jnp.concatenate(rows + [jnp.zeros((2, 128), jnp.int32)], 0)
            block = rows[0:SPARE]
            if tile:
                block = pltpu.roll(block, 128 - 32, 1)
            for k in range(1, 4):
                more = rows[SPARE * k : SPARE * (k + 1)]
                shift = (32 * k - 32 * tile) % 128
                if shift:
                    more = pltpu.roll(more, shift, 1)
                block = jnp.where(lane13 // 32 == k, more, block)
            steps_fine[tile, m, 0:SPARE] = block
    for h, part in enumerate(halves):
        steps_mid[SPARE * h : SPARE * (h + 1)] = part[HALF : HALF + SPARE]

    def load(tile, m):
        return pltpu.make_async_copy(steps_fine.at[tile, m], sm_fine.at[m], sm_sem.at[m])

    for m in range(STEPS):
        load(0, m).start()
    mid_lists = pltpu.make_async_copy(steps_mid, sm_mid, sm_sem.at[STEPS])
    mid_lists.start()

    for j in range(4):
        arrive(owners[j])
    for j in range(4):
        arrive_side(owners[j])
    for j in (4, 5, 6, 7, 0, 1, 2, 3):
        o = owners[j]
        for rel, there in ((1, None), (0, space > 0), (2, space < 31)):

            def take(rel=rel, o=o):
                piece = raw.at[rel, 1 - core, o]
                remote(piece, piece, twin_send.at[rel, o], twin_recv.at[rel, o], twin).wait_recv()
                fill(rel, 1 - core, o)

            if there is None:
                take()
            else:
                pl.when(there)(take)

    def product(source, place, targets, weights, acc):
        columns = []
        for q in range(WORDS):
            for h in range(2):
                picked = [source[place(q, h, t)] for t in range(targets)]
                columns.append(jnp.concatenate(picked, 0).astype(jnp.bfloat16))
        return acc + lax.dot_general(
            jnp.concatenate(columns, 1),
            weights,
            (((1,), (1,)), ((), ())),
            preferred_element_type=jnp.float32,
        )

    mid_lists.wait()
    acc = jnp.zeros((64, 128), jnp.float32)
    for m in range(STEPS):

        def place(q, h, t, m=m):
            word = m * WORDS + q
            return sm_mid[SPARE * h + word % SPARE, 8 * t + word // SPARE]

        acc = product(table_mid, place, 8, w_mid[m], acc)

    def in_order(panel, at):
        for half in range(4):
            first = at + 64 * (half // 2) + half % 2
            unpermuted[pl.ds(first, 32, 2), :] = panel[32 * half : 32 * half + 32]
        return unpermuted[at : at + 128]

    acc = in_order(jnp.concatenate([acc, jnp.zeros_like(acc)], 0).T, 0).T[0:64]
    level[...] = acc.astype(jnp.bfloat16)
    to_twin = remote(level, level_in, level_send.at[0], level_recv.at[0], twin)
    to_twin.start()

    def keep(rows, c):
        rows = rows.astype(jnp.float32)
        for j in range(8):
            table[MID_FINE + owners[j] * 2 + c] = rows[8 * j : 8 * j + 8]

    keep(level[...], core)

    def targets_of(tile, carry):
        acc = jnp.zeros((256, 128), jnp.float32)
        for m in range(STEPS):
            if m == STEPS - 1:

                @pl.when(tile == 0)
                def _():
                    to_twin.wait_recv()
                    keep(level_in[...], 1 - core)

            def place(q, h, t, m=m):
                at = WORDS * h + q
                return sm_fine[m, at % SPARE, 32 * (at // SPARE) + t]

            load(tile, m).wait()
            acc = product(table, place, 32, w_fine[m], acc)

            @pl.when(tile == 0)
            def _(m=m):
                load(1, m).start()

        result[tile] = acc.astype(jnp.bfloat16).reshape(4, 64, 128)
        for i in range(4):
            o = ((z_hi + 1 + tile) % 2) * 4 + (y + i) % 4

            def send(i=i, o=o):
                remote(
                    result.at[tile, i], result_in.at[own], out_send.at[4 * tile + i], out_recv.at[own], peer(o)
                ).start()

            if i == 0:
                pl.when(tile == 0)(send)
            else:
                send()
        return carry

    lax.fori_loop(0, 2, targets_of, 0)
    result_in[own] = result[1, 0]

    for j in (0, 1, 2, 3, 5, 6, 7):
        o = owners[j]
        remote(result.at[0, 0], result_in.at[o], out_send.at[j], out_recv.at[o], twin).wait_recv()
    for i in range(4):
        rows = []
        for g in range(8):
            both = result_in[g, 16 * i : 16 * i + 16].astype(jnp.float32)
            a, b = both[0:8], both[8:16]
            rows.append(jnp.where(low, a, pltpu.roll(b, 64, 1)))
            rows.append(jnp.where(low, pltpu.roll(a, 64, 1), b))
        panel = in_order(jnp.concatenate(rows, 0).T, 128 * i)
        out_ref[2 * i : 2 * i + 2] = panel.astype(jnp.bfloat16).reshape(2, 64, 128)

    to_twin.wait_send()
    for j in range(8):
        o = owners[j]
        piece = raw.at[1, core, o]
        if j != OWN:
            remote(words.at[o], words.at[o], list_send.at[o], list_recv.at[o], twin).wait_send()
            remote(piece, piece, a2a_send.at[o], a2a_recv.at[o], twin).wait_send()
            remote(result.at[0, 0], result_in.at[o], out_send.at[j], out_recv.at[o], twin).wait_send()
        remote(piece, piece, twin_send.at[1, o], twin_recv.at[1, o], twin).wait_send()
        for side, rel, there, back in ((0, 0, space < 31, space > 0), (1, 2, space > 0, space < 31)):

            @pl.when(there)
            def _(side=side, o=o, piece=piece):
                remote(piece, piece, side_send.at[side, o], side_recv.at[side, o], twin).wait_send()

            @pl.when(back)
            def _(rel=rel, o=o, piece=piece):
                remote(piece, piece, twin_send.at[rel, o], twin_recv.at[rel, o], twin).wait_send()


def body(parent, mid, fine, tmid, tfine, *rest):
    vmem = pl.BlockSpec(memory_space=pltpu.VMEM)
    hbm = pl.BlockSpec(memory_space=pl.ANY)
    bf16, f32, i32 = jnp.bfloat16, jnp.float32, jnp.int32
    dma = pltpu.SemaphoreType.DMA
    return pl.pallas_call(
        kernel,
        out_shape=jax.ShapeDtypeStruct((8, 64, 128), bf16),
        in_specs=[hbm] * 11,
        out_specs=vmem,
        scratch_shapes=[
            pltpu.VMEM((1, 64, 128), bf16),
            pltpu.VMEM((1, 64, 128), bf16),
            pltpu.VMEM((8, 64, 128), bf16),
            pltpu.VMEM((8, 64, 64), bf16),
            pltpu.VMEM((1, FAR), i32),
            pltpu.VMEM((8, FAR), i32),
            pltpu.SMEM((1,), i32),
            pltpu.SMEM((8,), i32),
            pltpu.SMEM((8,), i32),
            pltpu.VMEM((64, 64, FAR), bf16),
            pltpu.VMEM((64, 64, FAR), bf16),
            pltpu.VMEM((32 * 200, 128), f32),
            pltpu.VMEM((512, 64), f32),
            pltpu.VMEM((STEPS, 128, WORDS * 256), bf16),
            pltpu.VMEM((STEPS, 128, WORDS * 256), bf16),
            pltpu.VMEM((8, 80, 128), bf16),
            pltpu.VMEM((3, 2, 8, 80, 128), bf16),
            pltpu.VMEM((MID_FINE + 16, 8, 128), f32),
            pltpu.VMEM((PARENT_MID + 1, 8, 128), f32),
            pltpu.VMEM((16, 256), i32),
            pltpu.VMEM((8, 8, 128), i32),
            pltpu.VMEM((2, STEPS, 16, 128), i32),
            pltpu.VMEM((32, 128), i32),
            pltpu.VMEM((128, 128), f32),
            pltpu.VMEM((512, 128), f32),
            pltpu.VMEM((64, 128), bf16),
            pltpu.VMEM((64, 128), bf16),
            pltpu.VMEM((2, 4, 64, 128), bf16),
            pltpu.VMEM((8, 64, 128), bf16),
            pltpu.SMEM((STEPS, 16, 128), i32),
            pltpu.SMEM((32, 128), i32),
            dma((11,)),
            dma((STEPS + 1,)),
            dma((8,)),
            dma((8,)),
            dma((8,)),
            dma((8,)),
            dma((3, 8)),
            dma((3, 8)),
            dma((2, 8)),
            dma((2, 8)),
            dma((1,)),
            dma((1,)),
            dma((8,)),
            dma((8,)),
        ],
        compiler_params=pltpu.CompilerParams(
            collective_id=0, has_side_effects=True, vmem_limit_bytes=63 * 2**20
        ),
    )(parent, mid, fine, tmid.transpose(1, 2, 0), tfine.transpose(1, 2, 0), *rest)


def solution(mesh):
    placed = (
        P("space", None, None),
        P(("space", "sub"), None, None),
        P(("space", "sub"), None, None),
        P(),
        P(),
        P(),
        P(("space", "sub"), None),
        P(("space", "sub"), None),
        P(("space", "sub")),
        P(("space", "sub")),
        P(("space", "sub")),
    )
    return jax.shard_map(
        body, mesh=mesh, in_specs=placed, out_specs=P(("space", "sub"), None, None), check_vma=False
    )
```

```python
import functools

import jax
import jax.numpy as jnp
from jax import lax
from jax.experimental import pallas as pl
from jax.experimental.pallas import tpu as pltpu
from jax.sharding import PartitionSpec as P

MESH = pl.DeviceIdType.MESH
FAR = 189
SHIFT = 192
HALF = 100
STEPS, WORDS = 4, 25
SPARE = 13
ZERO_FINE, MID_FINE = 384, 385
ZERO_MID, PARENT_MID = 48, 49


def kernel(
    parent_hbm,
    mid_hbm,
    fine_hbm,
    tmid_hbm,
    tfine_hbm,
    shift_hbm,
    lmid_hbm,
    lfine_hbm,
    omid_hbm,
    ofine_hbm,
    pfine_hbm,
    out_ref,
    parent_ref,
    mid_ref,
    fine_ref,
    shift_ref,
    lmid_ref,
    lfine_ref,
    omid_ref,
    ofine_ref,
    pfine_ref,
    ops_fine,
    ops_mid,
    turned,
    shift_wide,
    w_fine,
    w_mid,
    stage,
    raw,
    table,
    table_mid,
    ext,
    words,
    steps_fine,
    steps_mid,
    flipped,
    unpermuted,
    level,
    level_in,
    result,
    result_in,
    sm_fine,
    sm_mid,
    op_sem,
    sm_sem,
    a2a_send,
    a2a_recv,
    list_send,
    list_recv,
    twin_send,
    twin_recv,
    side_send,
    side_recv,
    level_send,
    level_recv,
    out_send,
    out_recv,
):
    space = lax.axis_index("space")
    sub = lax.axis_index("sub")
    core = sub % 2
    group = sub // 2
    z_hi = group // 4
    y = group % 4
    twin = (space, group * 2 + 1 - core)

    owners = [(1 - z_hi) * 4 + (y + j) % 4 for j in range(4)]
    owners += [z_hi * 4 + (y + j) % 4 for j in range(4)]
    OWN = 4

    def peer(owner):
        return (space, owner * 2 + core)

    def remote(src, dst, send, recv, device):
        return pltpu.make_async_remote_copy(
            src_ref=src, dst_ref=dst, send_sem=send, recv_sem=recv, device_id=device, device_id_type=MESH
        )

    barrier = pltpu.get_barrier_semaphore()
    for j in range(8):
        if j != OWN:
            pl.semaphore_signal(barrier, inc=1, device_id=peer(owners[j]), device_id_type=MESH)
    pl.semaphore_signal(barrier, inc=1, device_id=twin, device_id_type=MESH)

    @pl.when(space > 0)
    def _():
        pl.semaphore_signal(barrier, inc=1, device_id=(space - 1, sub), device_id_type=MESH)

    @pl.when(space < 31)
    def _():
        pl.semaphore_signal(barrier, inc=1, device_id=(space + 1, sub), device_id_type=MESH)

    copies = (
        (fine_hbm, fine_ref),
        (mid_hbm, mid_ref),
        (lfine_hbm, lfine_ref),
        (lmid_hbm, lmid_ref),
        (omid_hbm, omid_ref),
        (ofine_hbm, ofine_ref),
        (pfine_hbm, pfine_ref),
        (parent_hbm, parent_ref),
        (shift_hbm, shift_ref),
        (tmid_hbm, ops_mid),
        (tfine_hbm, ops_fine),
    )
    copies = [pltpu.make_async_copy(a, b, op_sem.at[i]) for i, (a, b) in enumerate(copies)]
    for c in copies:
        c.start()
    for c in copies[:8]:
        c.wait()

    low = lax.broadcasted_iota(jnp.int32, (8, 128), 1) < 64
    for i in range(4):
        pair = fine_ref[2 * i : 2 * i + 2].reshape(128, 128).astype(jnp.float32).T
        for g in range(8):
            a = pair[16 * g : 16 * g + 8]
            b = pair[16 * g + 8 : 16 * g + 16]
            first = jnp.where(low, a, pltpu.roll(b, 64, 1))
            second = jnp.where(low, pltpu.roll(a, 64, 1), b)
            stage[g, 16 * i : 16 * i + 16] = jnp.concatenate([first, second], 0).astype(jnp.bfloat16)

    def doubled(panel):
        panel = panel.astype(jnp.float32)
        return jnp.concatenate([panel, panel], 0).T

    box = doubled(mid_ref[0])
    for g in range(8):
        rows = jnp.where(low, box[16 * g : 16 * g + 8], box[16 * g + 8 : 16 * g + 16])
        stage[g, 64:80] = jnp.concatenate([rows, jnp.zeros_like(rows)], 0).astype(jnp.bfloat16)
    flipped[...] = doubled(parent_ref[0])

    ext[0:8, 0:FAR] = lfine_ref[...]
    ext[8:9, 0:FAR] = lmid_ref[...]
    entry = ext[...]
    row = lax.broadcasted_iota(jnp.int32, (16, 256), 0)
    lane = lax.broadcasted_iota(jnp.int32, (16, 256), 1)
    octant = jnp.where(row == 8, omid_ref[0], -1)
    parent = jnp.where(row == 8, PARENT_MID, 0)
    for t in range(8):
        octant = jnp.where(row == t, ofine_ref[t], octant)
        parent = jnp.where(row == t, MID_FINE + jnp.clip(pfine_ref[t] - space * 16, 0, 15), parent)
    nothing = jnp.where(row < 8, ZERO_FINE, ZERO_MID)
    start = jnp.where(row < 8, (space - 1) * 128, (space - 1) * 16)
    last = jnp.where(row < 8, ZERO_FINE, ZERO_MID) - 1
    far = jnp.where(entry >= 0, jnp.clip(entry - start, 0, last), nothing)
    near = jnp.where(lane - SHIFT == octant, parent, nothing)
    rows = jnp.where(lane < FAR, far, near)
    packed = rows[:, :128] + pltpu.roll(rows, 256 - HALF, 1)[:, :128] * 65536
    fine_words = packed[0:8]
    mid_words = jnp.broadcast_to(packed[8:9], (8, 128))
    row8 = lax.broadcasted_iota(jnp.int32, (8, 128), 0)
    lane8 = lax.broadcasted_iota(jnp.int32, (8, 128), 1)
    spare = (lane8 >= HALF) & (lane8 < HALF + SPARE)
    for r in range(8):
        moved = pltpu.roll(mid_words, (HALF - SPARE * r) % 128, 1)
        fine_words = jnp.where(spare & (row8 == r), moved, fine_words)
    words[owners[OWN]] = fine_words

    pl.semaphore_wait(barrier, 8 + (space + 31) // 32 + (62 - space) // 32)

    own = owners[OWN]
    def send_list(o):
        remote(words.at[own], words.at[own], list_send.at[o], list_recv.at[own], peer(o)).start()

    def send_boxes(o):
        remote(stage.at[o], raw.at[1, core, own], a2a_send.at[o], a2a_recv.at[own], peer(o)).start()

    for j in range(4):
        send_list(owners[j])
    for j in range(4):
        send_boxes(owners[j])
    for j in (5, 6, 7):
        send_boxes(owners[j])
    for j in (5, 6, 7):
        send_list(owners[j])
    raw[1, core, own] = stage[own]

    def forward(o):
        piece = raw.at[1, core, o]
        remote(piece, piece, twin_send.at[1, o], twin_recv.at[1, o], twin).start()

        @pl.when(space < 31)
        def _():
            remote(
                piece, raw.at[0, core, o], side_send.at[0, o], side_recv.at[0, o], (space + 1, sub)
            ).start()

        @pl.when(space > 0)
        def _():
            remote(
                piece, raw.at[2, core, o], side_send.at[1, o], side_recv.at[1, o], (space - 1, sub)
            ).start()

    def fill(rel, c, o):
        first = rel * 128 + (o * 2 + c) * 8
        piece = raw[rel, c, o].astype(jnp.float32)
        table[pl.ds(first, 8)] = piece[0:64].reshape(8, 8, 128)
        mid = rel * 16 + o * 2 + c
        table_mid[mid] = piece[64:72]

    forward(own)
    fill(1, core, own)

    copies[8].wait()
    shift_wide[...] = shift_ref[...].astype(jnp.float32).reshape(512, 64)
    low32 = lax.broadcasted_iota(jnp.int32, (32, 128), 1) < 64

    def operators(ops, w):
        def turn(p, carry):
            both = ops[pl.ds(2 * p, 2)].reshape(128, FAR).astype(jnp.float32)
            at = pl.multiple_of(p * 200, 8)
            turned[pl.ds(at, 128), :] = both[:, 0:128].T
            turned[pl.ds(at + 128, FAR - 128), :] = both[:, 128:FAR].T
            return carry

        lax.fori_loop(0, 32, turn, 0)
        for c in range(FAR, SHIFT):
            turned[pl.ds(c, 32, 200), :] = jnp.zeros((32, 128), jnp.float32)
        for o in range(8):
            even = shift_wide[pl.ds(64 * o, 32, 2), :]
            odd = shift_wide[pl.ds(64 * o + 1, 32, 2), :]
            turned[pl.ds(SHIFT + o, 32, 200), :] = jnp.concatenate([even, odd], 1)

        def lay(m, carry):
            for q in range(WORDS):
                for h in range(2):
                    op = turned[pl.ds(m * WORDS + q + HALF * h, 32, 200), :]
                    swapped = pltpu.roll(op, 64, 1)
                    parts = [
                        jnp.where(low32, op, 0.0),
                        jnp.where(low32, swapped, 0.0),
                        jnp.where(low32, 0.0, swapped),
                        jnp.where(low32, 0.0, op),
                    ]
                    at = (2 * q + h) * 128
                    w[m, :, at : at + 128] = jnp.concatenate(parts, 0).astype(jnp.bfloat16)
            return carry

        lax.fori_loop(0, STEPS, lay, 0)

    copies[9].wait()
    operators(ops_mid, w_mid)

    table[ZERO_FINE] = jnp.zeros((8, 128), jnp.float32)
    table_mid[ZERO_MID] = jnp.zeros((8, 128), jnp.float32)
    at = pl.multiple_of(group * 16, 16)
    table_mid[PARENT_MID] = jnp.where(
        low, flipped[pl.ds(at, 8), :], flipped[pl.ds(at + 8, 8), :]
    )

    def arrive(o):
        piece = raw.at[1, core, o]
        remote(piece, piece, a2a_send.at[o], a2a_recv.at[o], twin).wait_recv()
        forward(o)
        fill(1, core, o)

    def arrive_side(o):
        for side, rel, there in ((0, 0, space > 0), (1, 2, space < 31)):

            @pl.when(there)
            def _(side=side, rel=rel):
                piece = raw.at[rel, core, o]
                remote(piece, piece, side_send.at[side, o], side_recv.at[side, o], twin).wait_recv()
                remote(piece, piece, twin_send.at[rel, o], twin_recv.at[rel, o], twin).start()
                fill(rel, core, o)

    for j in (5, 6, 7):
        arrive(owners[j])
    for j in (4, 5, 6, 7):
        arrive_side(owners[j])
    for j in range(4):
        arrive(owners[j])

    copies[10].wait()
    operators(ops_fine, w_fine)

    for j in range(8):
        if j != OWN:
            o = owners[j]
            remote(words.at[o], words.at[o], list_send.at[o], list_recv.at[o], twin).wait_recv()
    flat = jnp.concatenate([words[o] for o in owners] + [jnp.zeros((64, 128), jnp.int32)], 0).T
    lane13 = lax.broadcasted_iota(jnp.int32, (SPARE, 128), 1)
    halves = (flat & 0xFFFF, flat >> 16)
    for tile in range(2):
        for m in range(STEPS):
            rows = [v[m * WORDS : (m + 1) * WORDS] for v in halves]
            rows = jnp.concatenate(rows + [jnp.zeros((2, 128), jnp.int32)], 0)
            block = rows[0:SPARE]
            if tile:
                block = pltpu.roll(block, 128 - 32, 1)
            for k in range(1, 4):
                more = rows[SPARE * k : SPARE * (k + 1)]
                shift = (32 * k - 32 * tile) % 128
                if shift:
                    more = pltpu.roll(more, shift, 1)
                block = jnp.where(lane13 // 32 == k, more, block)
            steps_fine[tile, m, 0:SPARE] = block
    for h, part in enumerate(halves):
        steps_mid[SPARE * h : SPARE * (h + 1)] = part[HALF : HALF + SPARE]

    def load(tile, m):
        return pltpu.make_async_copy(steps_fine.at[tile, m], sm_fine.at[m], sm_sem.at[m])

    for m in range(STEPS):
        load(0, m).start()
    mid_lists = pltpu.make_async_copy(steps_mid, sm_mid, sm_sem.at[STEPS])
    mid_lists.start()

    for j in range(4):
        arrive_side(owners[j])
    for j in (4, 5, 6, 7, 0, 1, 2, 3):
        o = owners[j]
        for rel, there in ((1, None), (0, space > 0), (2, space < 31)):

            def take(rel=rel, o=o):
                piece = raw.at[rel, 1 - core, o]
                remote(piece, piece, twin_send.at[rel, o], twin_recv.at[rel, o], twin).wait_recv()
                fill(rel, 1 - core, o)

            if there is None:
                take()
            else:
                pl.when(there)(take)

    def product(source, place, targets, weights, acc):
        columns = []
        for q in range(WORDS):
            for h in range(2):
                picked = [source[place(q, h, t)] for t in range(targets)]
                columns.append(jnp.concatenate(picked, 0).astype(jnp.bfloat16))
        return acc + lax.dot_general(
            jnp.concatenate(columns, 1),
            weights,
            (((1,), (1,)), ((), ())),
            preferred_element_type=jnp.float32,
        )

    mid_lists.wait()
    acc = jnp.zeros((64, 128), jnp.float32)
    for m in range(STEPS):

        def place(q, h, t, m=m):
            word = m * WORDS + q
            return sm_mid[SPARE * h + word % SPARE, 8 * t + word // SPARE]

        acc = product(table_mid, place, 8, w_mid[m], acc)

    def in_order(panel, at):
        for half in range(4):
            first = at + 64 * (half // 2) + half % 2
            unpermuted[pl.ds(first, 32, 2), :] = panel[32 * half : 32 * half + 32]
        return unpermuted[at : at + 128]

    acc = in_order(jnp.concatenate([acc, jnp.zeros_like(acc)], 0).T, 0).T[0:64]
    level[...] = acc.astype(jnp.bfloat16)
    to_twin = remote(level, level_in, level_send.at[0], level_recv.at[0], twin)
    to_twin.start()

    def keep(rows, c):
        rows = rows.astype(jnp.float32)
        for j in range(8):
            table[MID_FINE + owners[j] * 2 + c] = rows[8 * j : 8 * j + 8]

    keep(level[...], core)

    def targets_of(tile, carry):
        acc = jnp.zeros((256, 128), jnp.float32)
        for m in range(STEPS):
            if m == STEPS - 1:

                @pl.when(tile == 0)
                def _():
                    to_twin.wait_recv()
                    keep(level_in[...], 1 - core)

            def place(q, h, t, m=m):
                at = WORDS * h + q
                return sm_fine[m, at % SPARE, 32 * (at // SPARE) + t]

            load(tile, m).wait()
            acc = product(table, place, 32, w_fine[m], acc)

            @pl.when(tile == 0)
            def _(m=m):
                load(1, m).start()

        result[tile] = acc.astype(jnp.bfloat16).reshape(4, 64, 128)
        for i in range(4):
            o = ((z_hi + 1 + tile) % 2) * 4 + (y + i) % 4

            def send(i=i, o=o):
                remote(
                    result.at[tile, i], result_in.at[own], out_send.at[4 * tile + i], out_recv.at[own], peer(o)
                ).start()

            if i == 0:
                pl.when(tile == 0)(send)
            else:
                send()
        return carry

    lax.fori_loop(0, 2, targets_of, 0)
    result_in[own] = result[1, 0]

    for j in (0, 1, 2, 3, 5, 6, 7):
        o = owners[j]
        remote(result.at[0, 0], result_in.at[o], out_send.at[j], out_recv.at[o], twin).wait_recv()
    for i in range(4):
        rows = []
        for g in range(8):
            both = result_in[g, 16 * i : 16 * i + 16].astype(jnp.float32)
            a, b = both[0:8], both[8:16]
            rows.append(jnp.where(low, a, pltpu.roll(b, 64, 1)))
            rows.append(jnp.where(low, pltpu.roll(a, 64, 1), b))
        panel = in_order(jnp.concatenate(rows, 0).T, 128 * i)
        out_ref[2 * i : 2 * i + 2] = panel.astype(jnp.bfloat16).reshape(2, 64, 128)

    to_twin.wait_send()
    for j in range(8):
        o = owners[j]
        piece = raw.at[1, core, o]
        if j != OWN:
            remote(words.at[o], words.at[o], list_send.at[o], list_recv.at[o], twin).wait_send()
            remote(piece, piece, a2a_send.at[o], a2a_recv.at[o], twin).wait_send()
            remote(result.at[0, 0], result_in.at[o], out_send.at[j], out_recv.at[o], twin).wait_send()
        remote(piece, piece, twin_send.at[1, o], twin_recv.at[1, o], twin).wait_send()
        for side, rel, there, back in ((0, 0, space < 31, space > 0), (1, 2, space > 0, space < 31)):

            @pl.when(there)
            def _(side=side, o=o, piece=piece):
                remote(piece, piece, side_send.at[side, o], side_recv.at[side, o], twin).wait_send()

            @pl.when(back)
            def _(rel=rel, o=o, piece=piece):
                remote(piece, piece, twin_send.at[rel, o], twin_recv.at[rel, o], twin).wait_send()


def body(parent, mid, fine, tmid, tfine, *rest):
    vmem = pl.BlockSpec(memory_space=pltpu.VMEM)
    hbm = pl.BlockSpec(memory_space=pl.ANY)
    bf16, f32, i32 = jnp.bfloat16, jnp.float32, jnp.int32
    dma = pltpu.SemaphoreType.DMA
    return pl.pallas_call(
        kernel,
        out_shape=jax.ShapeDtypeStruct((8, 64, 128), bf16),
        in_specs=[hbm] * 11,
        out_specs=vmem,
        scratch_shapes=[
            pltpu.VMEM((1, 64, 128), bf16),
            pltpu.VMEM((1, 64, 128), bf16),
            pltpu.VMEM((8, 64, 128), bf16),
            pltpu.VMEM((8, 64, 64), bf16),
            pltpu.VMEM((1, FAR), i32),
            pltpu.VMEM((8, FAR), i32),
            pltpu.SMEM((1,), i32),
            pltpu.SMEM((8,), i32),
            pltpu.SMEM((8,), i32),
            pltpu.VMEM((64, 64, FAR), bf16),
            pltpu.VMEM((64, 64, FAR), bf16),
            pltpu.VMEM((32 * 200, 128), f32),
            pltpu.VMEM((512, 64), f32),
            pltpu.VMEM((STEPS, 128, WORDS * 256), bf16),
            pltpu.VMEM((STEPS, 128, WORDS * 256), bf16),
            pltpu.VMEM((8, 80, 128), bf16),
            pltpu.VMEM((3, 2, 8, 80, 128), bf16),
            pltpu.VMEM((MID_FINE + 16, 8, 128), f32),
            pltpu.VMEM((PARENT_MID + 1, 8, 128), f32),
            pltpu.VMEM((16, 256), i32),
            pltpu.VMEM((8, 8, 128), i32),
            pltpu.VMEM((2, STEPS, 16, 128), i32),
            pltpu.VMEM((32, 128), i32),
            pltpu.VMEM((128, 128), f32),
            pltpu.VMEM((512, 128), f32),
            pltpu.VMEM((64, 128), bf16),
            pltpu.VMEM((64, 128), bf16),
            pltpu.VMEM((2, 4, 64, 128), bf16),
            pltpu.VMEM((8, 64, 128), bf16),
            pltpu.SMEM((STEPS, 16, 128), i32),
            pltpu.SMEM((32, 128), i32),
            dma((11,)),
            dma((STEPS + 1,)),
            dma((8,)),
            dma((8,)),
            dma((8,)),
            dma((8,)),
            dma((3, 8)),
            dma((3, 8)),
            dma((2, 8)),
            dma((2, 8)),
            dma((1,)),
            dma((1,)),
            dma((8,)),
            dma((8,)),
        ],
        compiler_params=pltpu.CompilerParams(
            collective_id=0, has_side_effects=True, vmem_limit_bytes=63 * 2**20
        ),
    )(parent, mid, fine, tmid.transpose(1, 2, 0), tfine.transpose(1, 2, 0), *rest)


def solution(mesh):
    placed = (
        P("space", None, None),
        P(("space", "sub"), None, None),
        P(("space", "sub"), None, None),
        P(),
        P(),
        P(),
        P(("space", "sub"), None),
        P(("space", "sub"), None),
        P(("space", "sub")),
        P(("space", "sub")),
        P(("space", "sub")),
    )
    return jax.shard_map(
        body, mesh=mesh, in_specs=placed, out_specs=P(("space", "sub"), None, None), check_vma=False
    )
```
